32 devices in a mesh: groups: 2 (over y), seq: 4 (over z), dp: 2 (over x), mp: 2 (over core).
Axes of the slice: x: 2, y: 2, z: 4, core: 2. Of those that a mesh axis runs over, the one named last changes fastest.
Arguments:
- features: bfloat16 [4, 16, 144, 1152], P(('groups', 'dp'), 'seq'), parts along dimension 0, may hold values from -6 to 6
- hidden_grad: bfloat16 [4, 256, 4, 1792], P(('groups', 'dp'), None, 'seq', 'mp'), parts along dimension 0, may hold values from -6 to 6
- weight: bfloat16 [1152, 1792], P(None, 'mp'), may hold values from -0.1875 to 0.1875
- bias: float32 [1792], P('mp'), may hold values from -4 to 4
- keep_count: int32 [4, 16], P(('groups', 'dp')), parts along dimension 0, may hold values from 1 to 144, as said below
- keep_order: int32 [4, 16, 144], P(('groups', 'dp'), 'seq'), parts along dimension 0, may hold values from 0 to 143, each once within a row
Outputs:
- grad_features: bfloat16 [4, 16, 144, 1152], P(('groups', 'dp'), 'seq', None, 'mp'), parts along dimension 0
- grad_weight: float32 [2304, 1792], P(('groups', 'seq', 'dp'), 'mp'), parts along dimension 0
The draws below stay inside these ranges and needn't reach their ends.
There are 2 independent parts, one for each index of `groups`. The reference program is written for one: setup_inputs(seed, part) draws one part's arguments, and reference() takes and returns one part's arrays. A program takes and returns all parts, laid end to end along the dimension named above; an argument that names none is the same for every part. Nothing has to cross between parts.
Inputs may be any that keep to these rules, and one draw needn't show every extreme that they name: `keep_count`: every frame keeps at least one token; a video keeps 1024 tokens in all; the 4 frames of one index of seq keep at most 576 tokens, and in every video one index of seq keeps exactly that many. `keep_order`: each frame's row is a permutation of 0 to 143.
All inputs are finite; a program needn't handle non-finite values.
Results may differ from the reference program's by a relative error of at most 0.0049.
Values may be sent and summed in bfloat16 or wider, within the bound.
No kernel may reach another device: no remote copies, remote signals or barrier semaphores. Data moves between devices by JAX's collectives and lax.ppermute only.
A program may use at most 64 MiB of HBM per device.

```python
import math
import jax
import jax.numpy as jnp
from jax import lax

DV = 1152
PH = 1792
PATCHES = 144
FR_DEV = 4
FRAMES = 16
SEQ_DEV = 256
KEPT = 1024
N_SEQ = 4
N_DP = 2


def draw_keep_count(key, part):
    key = jax.random.fold_in(key, 11)
    key_heavy, key_perm, key_moves = jax.random.split(key, 3)
    others = FRAMES - FR_DEV
    rest_total = KEPT - FR_DEV * PATCHES
    base_count = rest_total // others
    extra_count = rest_total - base_count * others
    spread_max = max(0, min(base_count - 1, PATCHES - base_count - 1))
    heavy_block = jax.random.randint(key_heavy, (N_DP,), 0, N_SEQ)
    perm_keys = jax.random.split(key_perm, N_DP)
    rank_pos = jax.vmap(lambda sub_key: jax.random.permutation(sub_key, others))(perm_keys)
    moves = jax.random.randint(key_moves, (N_DP, others // 2 + 1), -spread_max, spread_max + 1)
    pair_index = rank_pos // 2
    sign_value = 1 - 2 * (rank_pos % 2)
    unpaired = (rank_pos >= 2 * (others // 2)).astype(jnp.int32)
    shift_value = jnp.take_along_axis(moves, pair_index, axis=1) * sign_value * (1 - unpaired)
    other_count = base_count + (rank_pos < extra_count).astype(jnp.int32) + shift_value
    frame_ids = jnp.arange(FRAMES, dtype=jnp.int32)
    heavy_start = heavy_block[:, None] * FR_DEV
    is_heavy = frame_ids[None, :] // FR_DEV == heavy_block[:, None]
    rank_index = jnp.where(frame_ids[None, :] < heavy_start, frame_ids[None, :], frame_ids[None, :] - FR_DEV)
    rank_index = jnp.clip(rank_index, 0, others - 1)
    counts = jnp.where(is_heavy, PATCHES, jnp.take_along_axis(other_count, rank_index, axis=1))
    return counts.astype(jnp.int32)


def steps_of(own_key, extent, cuts, low, high):
    level, own = 1.0, jax.random.fold_in(own_key, 6)
    for dim, blocks in cuts:
        heights = jnp.exp(jax.random.uniform(jax.random.fold_in(own, dim), (blocks,), jnp.float32, low / len(cuts), high / len(cuts)))
        level = level * jnp.repeat(heights, extent[dim] // blocks).reshape([-1 if axis == dim else 1 for axis in range(len(extent))])
    return level


def normal_values(own_key, extent, width, bound, pieces=(), kind=jnp.bfloat16):
    entries = width * jax.random.normal(own_key, extent, jnp.float32)
    if pieces:
        entries = entries * steps_of(own_key, extent, pieces, -0.22, 0.18)
    return jnp.clip(entries, -bound, bound).astype(kind)


def setup_inputs(seed: int = 0, part: int = 0) -> dict:
    streams_of = jax.random.split(jax.random.key(seed), 7)
    part_splits = jax.random.split(jax.random.fold_in(streams_of[6], part), 7)
    features = normal_values(part_splits[0], (N_DP, FRAMES, PATCHES, DV), 1.0, 6.0, ((0, 2), (1, 4)))
    hidden_grad = normal_values(part_splits[1], (N_DP, SEQ_DEV, N_SEQ, PH), 1.0, 6.0, ((0, 2), (2, 4), (3, 2)))
    weight = normal_values(streams_of[2], (DV, PH), DV ** -0.5, 0.1875, ((1, 2),))
    bias = normal_values(streams_of[3], (PH,), 1.0, 4.0, ((0, 2),), jnp.float32)
    keep_count = draw_keep_count(jax.random.fold_in(jax.random.fold_in(streams_of[6], part), 71), part)
    keep_order = jax.vmap(lambda own: jax.random.permutation(own, PATCHES))(jax.random.split(part_splits[5], N_DP * FRAMES)).reshape((N_DP, FRAMES, PATCHES)).astype(jnp.int32)
    return dict(features=features, hidden_grad=hidden_grad, weight=weight, bias=bias, keep_count=keep_count, keep_order=keep_order)


inv_root_two = 0.7071067811865476
inv_root_tau = 0.3989422804014327

def gelu_slope(preact):
    return 0.5 * (1.0 + lax.erf(preact * inv_root_two)) + preact * jnp.exp(-0.5 * preact * preact) * inv_root_tau

def reference(features, hidden_grad, weight, bias, keep_count, keep_order):
    grad_sum = jnp.zeros((DV, PH), jnp.float32)
    position = jnp.arange(KEPT, dtype=jnp.int32)
    outputs = []
    for video_index in range(N_DP):
        counts = keep_count[video_index].astype(jnp.int32)
        start = (jnp.cumsum(counts) - counts).astype(jnp.int32)
        marker = jnp.zeros((KEPT,), jnp.int32).at[start[1:]].add(1)
        frame_id = jnp.cumsum(marker).astype(jnp.int32)
        within = (position - start[frame_id]).astype(jnp.int32)
        token_id = keep_order[video_index][frame_id, within].astype(jnp.int32)
        seq_rows = features[video_index][frame_id, token_id]
        seq_grads = hidden_grad[video_index].reshape(KEPT, PH)
        preact = jnp.dot(seq_rows, weight, preferred_element_type=jnp.float32) + bias
        slope_grad = (seq_grads.astype(jnp.float32) * gelu_slope(preact)).astype(jnp.bfloat16)
        grad_sum = grad_sum + jnp.dot(seq_rows.T, slope_grad, preferred_element_type=jnp.float32)
        back_rows = jnp.dot(slope_grad, weight.T, preferred_element_type=jnp.float32).astype(jnp.bfloat16)
        dense_index = (frame_id * PATCHES + token_id).astype(jnp.int32)
        dense_rows = jnp.zeros((FRAMES * PATCHES, DV), back_rows.dtype).at[dense_index].set(back_rows)
        outputs.append(dense_rows.reshape(FRAMES, PATCHES, DV))
    grad_weight = grad_sum * (1.0 / math.sqrt(N_DP * KEPT))
    return (jnp.stack(outputs), grad_weight)
```

```python
import functools
import math

import jax
import jax.numpy as jnp
from jax import lax
from jax.experimental import pallas as pl
from jax.experimental.pallas import tpu as pltpu
from jax.sharding import PartitionSpec as P

inv_root_two = 0.7071067811865476
inv_root_tau = 0.3989422804014327
bf16, f32, i32 = jnp.bfloat16, jnp.float32, jnp.int32
vmem = pl.BlockSpec(memory_space=pltpu.VMEM)
smem = pl.BlockSpec(memory_space=pltpu.SMEM)


def call(body, outs, in_specs, scratch=(), flops=0, moved=0, exps=0):
    return pl.pallas_call(
        body,
        out_shape=outs,
        in_specs=in_specs,
        out_specs=[vmem] * len(outs),
        scratch_shapes=list(scratch),
        compiler_params=pltpu.CompilerParams(vmem_limit_bytes=40 << 20),
        cost_estimate=pl.CostEstimate(flops=flops, bytes_accessed=moved, transcendentals=exps),
    )


def shape(dtype, *extent):
    return jax.ShapeDtypeStruct(extent, dtype)


def exchanged(array, axis, distance):
    return lax.ppermute(array, axis, [(i, i ^ distance) for i in range(lax.axis_size(axis))])


def gelu_slope(preact):
    return (
        0.5 * (1.0 + lax.erf(preact * inv_root_two))
        + preact * jnp.exp(-0.5 * preact * preact) * inv_root_tau
    )


def kept_before(count_ref, frame):
    total = jnp.int32(0)
    for index in range(count_ref.shape[1]):
        total += jnp.where(index < frame, count_ref[0, index], 0)
    return total


def slot_start(range_begin, source, seq_size, rows_dev, slot_rows):
    first_row = lax.div(range_begin - source + (seq_size - 1), jnp.int32(seq_size))
    return jnp.minimum(first_row, rows_dev - slot_rows)


def pack_kernel(seq_size, frames_dev, slot_rows, partner, count_ref, grads_ref, *outs):
    my_seq = lax.axis_index("seq")
    rows_dev = grads_ref.shape[0]
    row = lax.broadcasted_iota(i32, (slot_rows, rows_dev), 0)
    column = lax.broadcasted_iota(i32, (slot_rows, rows_dev), 1)
    for k in range(seq_size):
        target = partner(my_seq, k)
        start = slot_start(kept_before(count_ref, target * frames_dev), my_seq, seq_size, rows_dev, slot_rows)
        picks = jnp.where(column == row + start, 1.0, 0.0).astype(bf16)
        rows = jnp.dot(picks, grads_ref[...], preferred_element_type=f32).astype(bf16)
        if len(outs) == 1:
            outs[0][k] = rows
        else:
            outs[k][...] = rows


def slope_kernel(
    seq_size, rows_dev, slot_rows, partner, count_ref, order_ref, tokens_ref, weight_ref, bias_ref,
    slope_ref, rows_t_ref, place_ref, slot_pos, token_pos, rows_ref,
):
    my_seq = lax.axis_index("seq")
    frames_dev, patches = order_ref.shape
    tokens, width = tokens_ref.shape
    slots = slope_ref.shape[0]
    range_begin = kept_before(count_ref, my_seq * frames_dev)
    step = lax.broadcasted_iota(i32, (slot_rows, 1), 0)
    lane = lax.broadcasted_iota(i32, (1, slots), 1)
    slot_row = jnp.zeros((1, slots), i32)
    for k in range(seq_size):
        source = partner(my_seq, k)
        start = slot_start(range_begin, source, seq_size, rows_dev, slot_rows)
        slot_pos[k * slot_rows:(k + 1) * slot_rows, :] = (start + step) * seq_size + source
        slot_row = jnp.where(lane >= k * slot_rows, (start + lane - k * slot_rows) * seq_size + source, slot_row)
    token = lax.broadcasted_iota(i32, (patches, patches), 0)
    index = lax.broadcasted_iota(i32, (patches, patches), 1)
    begin = range_begin
    for frame in range(frames_dev):
        count = count_ref[0, my_seq * frames_dev + frame]
        order = order_ref[frame:frame + 1, :]
        rank = jnp.sum(jnp.where(order == token, index, 0), axis=1, keepdims=True)
        token_pos[frame * patches:(frame + 1) * patches, :] = jnp.where(rank < count, rank + begin, -1)
        begin += count
    column = token_pos[...]
    place_ref[...] = jnp.where(column == slot_row, 1.0, 0.0).astype(bf16)
    row = lax.broadcasted_iota(i32, (tokens, tokens), 0)
    lane = lax.broadcasted_iota(i32, (tokens, tokens), 1)
    token_row = jnp.sum(jnp.where(row == lane, column, 0), axis=0, keepdims=True)
    block = slots // 4

    @pl.loop(0, 4)
    def _(part):
        here = pl.ds(pl.multiple_of(part * block, 16), block)
        picks = jnp.where(slot_pos[here, :] == token_row, 1.0, 0.0).astype(bf16)
        rows = jnp.dot(picks, tokens_ref[...], preferred_element_type=f32).astype(bf16)
        rows_ref[here, :] = rows
        preact = jnp.dot(rows, weight_ref[...], preferred_element_type=f32) + bias_ref[...]
        slope_ref[here, :] = gelu_slope(preact)

    rows_t_ref[...] = rows_ref[...].T


def grad_kernel(chunks, tile, slots_in, *refs):
    grads, (slope_ref, rows_t_ref, grad_ref), outs = refs[:slots_in], refs[slots_in:slots_in + 3], refs[slots_in + 3:]
    slot_rows = grads[0].shape[0]
    for k, ref in enumerate(grads):
        here = slice(k * slot_rows, (k + 1) * slot_rows)
        grad_ref[here, :] = (ref[...].astype(f32) * slope_ref[here, :]).astype(bf16)
    weight_tiles(chunks, tile, rows_t_ref, grad_ref, outs)


def weight_tiles(chunks, tile, rows_t_ref, grad_ref, outs):
    my_seq, my_dp = lax.axis_index("seq"), lax.axis_index("dp")
    videos = lax.axis_size("dp")
    for (k, j), ref in zip(chunks, outs):
        owner = (my_seq ^ k) * videos + (my_dp ^ j)
        rows = rows_t_ref[pl.ds(pl.multiple_of(owner * tile, 16), tile), :]
        ref[...] = jnp.dot(rows, grad_ref[...], preferred_element_type=f32).astype(ref.dtype)


def tiles_kernel(chunks, tile, rows_t_ref, grad_ref, *outs):
    weight_tiles(chunks, tile, rows_t_ref, grad_ref, outs)


def row_kernel(grad_ref, weight_ref, own_ref, peer_ref):
    my_half = lax.axis_index("mp")
    half = own_ref.shape[1]
    for ref, which in ((peer_ref, 1 - my_half), (own_ref, my_half)):
        part = weight_ref[pl.ds(pl.multiple_of(which * half, 16), half), :]
        ref[...] = lax.dot_general(grad_ref[...], part, (((1,), (1,)), ((), ())), preferred_element_type=f32)


def place_kernel(own_ref, peer_ref, place_ref, out_ref):
    rows = (own_ref[...] + peer_ref[...]).astype(bf16)
    out_ref[...] = jnp.dot(place_ref[...], rows, preferred_element_type=f32).astype(bf16)


def shards(features, hidden_grad, weight, bias, keep_count, keep_order):
    seq_size, videos = lax.axis_size("seq"), lax.axis_size("dp")
    frames_dev, patches, width = features.shape[1:]
    rows_dev, hidden = hidden_grad.shape[1], hidden_grad.shape[3]
    tokens = frames_dev * patches
    slot_rows = (tokens + seq_size - 1) // seq_size
    slot_rows = (slot_rows + 15) // 16 * 16
    slots = seq_size * slot_rows
    tile = width // (seq_size * videos)
    direct = seq_size <= 8 and videos <= 2 and tile % 16 == 0
    norm_scale = 1.0 / math.sqrt(videos * seq_size * rows_dev)

    def partner(me, k):
        return me ^ k if direct else jnp.int32(k)

    local_grads = hidden_grad.reshape(rows_dev, hidden)
    flat_tokens = features.reshape(tokens, width)
    one = shape(bf16, slot_rows, hidden)
    outgoing = call(
        functools.partial(pack_kernel, seq_size, frames_dev, slot_rows, partner),
        [one] * seq_size if direct else [shape(bf16, seq_size, slot_rows, hidden)],
        [smem, vmem],
        flops=2 * slots * rows_dev * hidden,
        moved=2 * hidden * (rows_dev + slots),
    )(keep_count, local_grads)
    if direct:
        arrived = [exchanged(rows, "seq", k) if k else rows for k, rows in enumerate(outgoing)]
    else:
        arrived = [lax.all_to_all(outgoing[0], "seq", split_axis=0, concat_axis=0, tiled=True).reshape(slots, hidden)]

    slope, rows_t, place = call(
        functools.partial(slope_kernel, seq_size, rows_dev, slot_rows, partner),
        [shape(f32, slots, hidden), shape(bf16, width, slots), shape(bf16, tokens, slots)],
        [smem, vmem, vmem, vmem, vmem],
        [pltpu.VMEM((slots, 1), i32), pltpu.VMEM((tokens, 1), i32), pltpu.VMEM((slots, width), bf16)],
        flops=2 * slots * width * (tokens + hidden),
        moved=2 * width * (tokens + hidden + slots) + 4 * slots * hidden,
        exps=2 * slots * hidden,
    )(keep_count, keep_order.reshape(frames_dev, patches), flat_tokens, weight, bias.reshape(1, hidden))

    order = [k for k in range(seq_size - 1, -1, -1)]
    sent = [(k, 1) for k in order] if direct and videos == 2 else []
    own = [(k, 0) for k in order] if direct else []
    tile_flops, tile_bytes = 2 * tile * slots * hidden, 4 * tile * hidden
    slope_grad, *first = call(
        functools.partial(grad_kernel, sent[:1], tile, len(arrived)),
        [shape(bf16, slots, hidden)] + [shape(bf16, tile, hidden)] * len(sent[:1]),
        [vmem] * (len(arrived) + 2),
        flops=tile_flops,
        moved=8 * slots * hidden + 2 * slots * width,
    )(*arrived, slope, rows_t)
    if direct:
        rest = call(
            functools.partial(tiles_kernel, sent[1:], tile),
            [shape(bf16, tile, hidden)] * len(sent[1:]),
            [vmem, vmem],
            flops=tile_flops * len(sent[1:]),
            moved=tile_bytes * len(sent[1:]),
        )(rows_t, slope_grad) if sent[1:] else []
        mine = call(
            functools.partial(tiles_kernel, own, tile),
            [shape(f32, tile, hidden)] * len(own),
            [vmem, vmem],
            flops=tile_flops * len(own),
            moved=tile_bytes * len(own),
        )(rows_t, slope_grad)
        from_dp = [exchanged(part, "dp", 1) for part in first + list(rest)]
        sums = [part + peer.astype(f32) for part, peer in zip(mine, from_dp)] if sent else mine
        summed = sums[-1]
        for k, part in zip(order[:-1], sums[:-1]):
            summed = summed + exchanged(part.astype(bf16), "seq", k).astype(f32)
    else:
        partial = jnp.dot(rows_t, slope_grad, preferred_element_type=f32)
        summed = lax.psum_scatter(partial, ("seq", "dp"), scatter_dimension=0, tiled=True)

    half = width // lax.axis_size("mp")
    own_part, peer_part = call(
        row_kernel,
        [shape(f32, slots, half)] * 2,
        [vmem, vmem],
        flops=2 * slots * width * hidden,
        moved=2 * hidden * (slots + width) + 4 * slots * width,
    )(slope_grad, weight)
    peer_part = exchanged(peer_part, "mp", 1)
    (grid,) = call(
        place_kernel,
        [shape(bf16, tokens, half)],
        [vmem] * 3,
        flops=2 * tokens * slots * half,
        moved=2 * tokens * (slots + half) + 8 * slots * half,
    )(own_part, peer_part, place)
    return (grid.reshape(1, frames_dev, patches, half), summed * norm_scale)


def solution(mesh):
    return jax.shard_map(
        shards,
        mesh=mesh,
        in_specs=(
            P(("groups", "dp"), "seq", None, None),
            P(("groups", "dp"), None, "seq", "mp"),
            P(None, "mp"),
            P("mp"),
            P(("groups", "dp"), None),
            P(("groups", "dp"), "seq", None),
        ),
        out_specs=(P(("groups", "dp"), "seq", None, "mp"), P(("groups", "seq", "dp"), "mp")),
        check_vma=False,
    )
```

```python
import functools
import math

import jax
import jax.numpy as jnp
from jax import lax
from jax.experimental import pallas as pl
from jax.experimental.pallas import tpu as pltpu
from jax.sharding import PartitionSpec as P

inv_root_two = 0.7071067811865476
inv_root_tau = 0.3989422804014327
bf16, f32, i32 = jnp.bfloat16, jnp.float32, jnp.int32
vmem = pl.BlockSpec(memory_space=pltpu.VMEM)
smem = pl.BlockSpec(memory_space=pltpu.SMEM)
hbm = pl.BlockSpec(memory_space=pltpu.HBM)


def call(body, outs, in_specs, scratch=(), flops=0, moved=0, exps=0):
    return pl.pallas_call(
        body,
        out_shape=outs,
        in_specs=in_specs,
        out_specs=[vmem] * len(outs),
        scratch_shapes=list(scratch),
        compiler_params=pltpu.CompilerParams(vmem_limit_bytes=40 << 20),
        cost_estimate=pl.CostEstimate(flops=flops, bytes_accessed=moved, transcendentals=exps),
    )


def shape(dtype, *extent):
    return jax.ShapeDtypeStruct(extent, dtype)


def exchanged(array, axis, distance):
    return lax.ppermute(array, axis, [(i, i ^ distance) for i in range(lax.axis_size(axis))])


def gelu_slope(preact):
    return (
        0.5 * (1.0 + lax.erf(preact * inv_root_two))
        + preact * jnp.exp(-0.5 * preact * preact) * inv_root_tau
    )


def kept_before(count_ref, frame):
    total = jnp.int32(0)
    for index in range(count_ref.shape[1]):
        total += jnp.where(index < frame, count_ref[0, index], 0)
    return total


def slot_start(range_begin, source, seq_size, rows_dev, slot_rows):
    first_row = lax.div(range_begin - source + (seq_size - 1), jnp.int32(seq_size))
    return jnp.minimum(first_row, rows_dev - slot_rows)


def pack_kernel(seq_size, frames_dev, slot_rows, partner, count_hbm, grads_hbm, *refs):
    *outs, count_ref, grads_ref, count_sem, grads_sem = refs
    count_copy = pltpu.make_async_copy(count_hbm, count_ref, count_sem)
    grads_copy = pltpu.make_async_copy(grads_hbm, grads_ref, grads_sem)
    count_copy.start()
    grads_copy.start()
    count_copy.wait()
    my_seq = lax.axis_index("seq")
    rows_dev = grads_ref.shape[0]
    row = lax.broadcasted_iota(i32, (slot_rows, rows_dev), 0)
    column = lax.broadcasted_iota(i32, (slot_rows, rows_dev), 1)
    starts = []
    for k in range(seq_size):
        begin = kept_before(count_ref, partner(my_seq, k) * frames_dev)
        starts.append(slot_start(begin, my_seq, seq_size, rows_dev, slot_rows))
    grads_copy.wait()
    for k, start in enumerate(starts):
        picks = jnp.where(column == row + start, 1.0, 0.0).astype(bf16)
        rows = jnp.dot(picks, grads_ref[...], preferred_element_type=f32).astype(bf16)
        if len(outs) == 1:
            outs[0][k] = rows
        else:
            outs[k][...] = rows


def slope_kernel(
    seq_size, rows_dev, slot_rows, partner, count_ref, order_ref, tokens_ref, weight_ref, bias_ref,
    slope_ref, rows_t_ref, place_ref, slot_pos, token_pos, rows_ref,
):
    my_seq = lax.axis_index("seq")
    frames_dev, patches = order_ref.shape
    tokens, width = tokens_ref.shape
    slots = slope_ref.shape[0]
    range_begin = kept_before(count_ref, my_seq * frames_dev)
    step = lax.broadcasted_iota(i32, (slot_rows, 1), 0)
    lane = lax.broadcasted_iota(i32, (1, slots), 1)
    slot_row = jnp.zeros((1, slots), i32)
    for k in range(seq_size):
        source = partner(my_seq, k)
        start = slot_start(range_begin, source, seq_size, rows_dev, slot_rows)
        slot_pos[k * slot_rows:(k + 1) * slot_rows, :] = (start + step) * seq_size + source
        slot_row = jnp.where(lane >= k * slot_rows, (start + lane - k * slot_rows) * seq_size + source, slot_row)
    token = lax.broadcasted_iota(i32, (patches, patches), 0)
    index = lax.broadcasted_iota(i32, (patches, patches), 1)
    begin = range_begin
    for frame in range(frames_dev):
        count = count_ref[0, my_seq * frames_dev + frame]
        order = order_ref[frame:frame + 1, :]
        rank = jnp.sum(jnp.where(order == token, index, 0), axis=1, keepdims=True)
        token_pos[frame * patches:(frame + 1) * patches, :] = jnp.where(rank < count, rank + begin, -1)
        begin += count
    column = token_pos[...]
    place_ref[...] = jnp.where(column == slot_row, 1.0, 0.0).astype(bf16)
    row = lax.broadcasted_iota(i32, (tokens, tokens), 0)
    lane = lax.broadcasted_iota(i32, (tokens, tokens), 1)
    token_row = jnp.sum(jnp.where(row == lane, column, 0), axis=0, keepdims=True)
    block = slots // 4

    @pl.loop(0, 4)
    def _(part):
        here = pl.ds(pl.multiple_of(part * block, 16), block)
        picks = jnp.where(slot_pos[here, :] == token_row, 1.0, 0.0).astype(bf16)
        rows = jnp.dot(picks, tokens_ref[...], preferred_element_type=f32).astype(bf16)
        rows_ref[here, :] = rows
        preact = jnp.dot(rows, weight_ref[...], preferred_element_type=f32) + bias_ref[...]
        slope_ref[here, :] = gelu_slope(preact)

    rows_t_ref[...] = rows_ref[...].T


def grad_kernel(slots_in, chunks, tile, *refs):
    grads, (slope_ref, rows_t_ref, grad_ref), outs = refs[:slots_in], refs[slots_in:slots_in + 3], refs[slots_in + 3:]
    slot_rows = grads[0].shape[0]
    for k, ref in enumerate(grads):
        here = slice(k * slot_rows, (k + 1) * slot_rows)
        grad_ref[here, :] = (ref[...].astype(f32) * slope_ref[here, :]).astype(bf16)
    weight_rows(chunks, tile, rows_t_ref, grad_ref, outs)


def weight_rows(chunks, tile, rows_t_ref, grad_ref, outs):
    my_seq, my_dp = lax.axis_index("seq"), lax.axis_index("dp")
    videos = lax.axis_size("dp")
    for (k, j, first, last), ref in zip(chunks, outs):
        owner = (my_seq ^ k) * videos + (my_dp ^ j)
        rows = rows_t_ref[pl.ds(pl.multiple_of(owner * tile + first, 16), last - first), :]
        ref[...] = jnp.dot(rows, grad_ref[...], preferred_element_type=f32).astype(ref.dtype)


def rows_kernel(chunks, tile, rows_t_ref, grad_ref, *outs):
    weight_rows(chunks, tile, rows_t_ref, grad_ref, outs)


def row_kernel(grad_ref, weight_ref, own_ref, peer_ref):
    my_half = lax.axis_index("mp")
    half = own_ref.shape[1]
    for ref, which in ((peer_ref, 1 - my_half), (own_ref, my_half)):
        part = weight_ref[pl.ds(pl.multiple_of(which * half, 16), half), :]
        rows = lax.dot_general(grad_ref[...], part, (((1,), (1,)), ((), ())), preferred_element_type=f32)
        ref[...] = rows.astype(ref.dtype)


def place_kernel(own_ref, peer_ref, place_ref, out_ref):
    rows = (own_ref[...] + peer_ref[...].astype(f32)).astype(bf16)
    out_ref[...] = jnp.dot(place_ref[...], rows, preferred_element_type=f32).astype(bf16)


def shards(features, hidden_grad, weight, bias, keep_count, keep_order):
    seq_size, videos = lax.axis_size("seq"), lax.axis_size("dp")
    frames_dev, patches, width = features.shape[1:]
    rows_dev, hidden = hidden_grad.shape[1], hidden_grad.shape[3]
    tokens = frames_dev * patches
    slot_rows = (tokens + seq_size - 1) // seq_size
    slot_rows = (slot_rows + 15) // 16 * 16
    slots = seq_size * slot_rows
    tile = width // (seq_size * videos)
    direct = seq_size == 4 and videos == 2 and tile % 48 == 0
    norm_scale = 1.0 / math.sqrt(videos * seq_size * rows_dev)

    def partner(me, k):
        return me ^ k if direct else jnp.int32(k)

    local_grads = hidden_grad.reshape(rows_dev, hidden)
    flat_tokens = features.reshape(tokens, width)
    one = shape(bf16, slot_rows, hidden)
    outgoing = call(
        functools.partial(pack_kernel, seq_size, frames_dev, slot_rows, partner),
        [one] * seq_size if direct else [shape(bf16, seq_size, slot_rows, hidden)],
        [hbm, hbm],
        [
            pltpu.SMEM(keep_count.shape, i32),
            pltpu.VMEM((rows_dev, hidden), bf16),
            pltpu.SemaphoreType.DMA(()),
            pltpu.SemaphoreType.DMA(()),
        ],
        flops=2 * slots * rows_dev * hidden,
        moved=2 * hidden * (rows_dev + slots),
    )(keep_count, local_grads)
    if direct:
        arrived = [exchanged(rows, "seq", k) if k else rows for k, rows in enumerate(outgoing)]
    else:
        arrived = [lax.all_to_all(outgoing[0], "seq", split_axis=0, concat_axis=0, tiled=True).reshape(slots, hidden)]

    slope, rows_t, place = call(
        functools.partial(slope_kernel, seq_size, rows_dev, slot_rows, partner),
        [shape(f32, slots, hidden), shape(bf16, width, slots), shape(bf16, tokens, slots)],
        [smem, vmem, vmem, vmem, vmem],
        [pltpu.VMEM((slots, 1), i32), pltpu.VMEM((tokens, 1), i32), pltpu.VMEM((slots, width), bf16)],
        flops=2 * slots * width * (tokens + hidden),
        moved=2 * width * (tokens + hidden + slots) + 4 * slots * hidden,
        exps=2 * slots * hidden,
    )(keep_count, keep_order.reshape(frames_dev, patches), flat_tokens, weight, bias.reshape(1, hidden))

    wide = shape(bf16, slots, hidden)
    spans = [(3, 0, tile), (2, 0, tile), (1, 0, tile), (0, 0, tile)] if direct else []

    def weight_part(body, chunks, dtypes, operands, extra=()):
        rows = sum(last - first for _, _, first, last in chunks)
        return call(
            functools.partial(body, chunks, tile),
            list(extra) + [shape(dtype, last - first, hidden) for dtype, (_, _, first, last) in zip(dtypes, chunks)],
            [vmem] * len(operands),
            flops=2 * rows * slots * hidden,
            moved=4 * rows * hidden + 2 * slots * (rows + hidden),
        )(*operands)

    sent = [(k, 1, first, last) for k, first, last in spans]
    own = [(k, 0, first, last) for k, first, last in spans]
    slope_grad, *to_dp = weight_part(
        functools.partial(grad_kernel, len(arrived)), sent[:1], [bf16], [*arrived, slope, rows_t], [wide]
    )
    if direct:
        to_dp += weight_part(rows_kernel, sent[1:], [bf16] * 3, [rows_t, slope_grad])
        far, second, near, home = weight_part(rows_kernel, own, [f32] * 4, [rows_t, slope_grad])
        got, home_out = lax.optimization_barrier((exchanged(to_dp[0], "dp", 1), to_dp[3]))
        far = exchanged((far + got.astype(f32)).astype(bf16), "seq", 3)
        second = exchanged((second + exchanged(to_dp[1], "dp", 1).astype(f32)).astype(bf16), "seq", 2)
        near = exchanged((near + exchanged(to_dp[2], "dp", 1).astype(f32)).astype(bf16), "seq", 1)
        home = home + exchanged(home_out, "dp", 1).astype(f32)
    else:
        partial = jnp.dot(rows_t, slope_grad, preferred_element_type=f32)
        summed = lax.psum_scatter(partial, ("seq", "dp"), scatter_dimension=0, tiled=True)

    half = width // lax.axis_size("mp")
    own_part, peer_part = call(
        row_kernel,
        [shape(f32, slots, half), shape(bf16, slots, half)],
        [vmem, vmem],
        flops=2 * slots * width * hidden,
        moved=2 * hidden * (slots + width) + 4 * slots * width,
    )(slope_grad, weight)
    peer_part = exchanged(peer_part, "mp", 1)
    (grid,) = call(
        place_kernel,
        [shape(bf16, tokens, half)],
        [vmem] * 3,
        flops=2 * tokens * slots * half,
        moved=2 * tokens * (slots + half) + 8 * slots * half,
    )(own_part, peer_part, place)
    if direct:
        home, grid = lax.optimization_barrier((home, grid))
        summed = home + far.astype(f32) + second.astype(f32) + near.astype(f32)
    return (grid.reshape(1, frames_dev, patches, half), summed * norm_scale)


def solution(mesh):
    return jax.shard_map(
        shards,
        mesh=mesh,
        in_specs=(
            P(("groups", "dp"), "seq", None, None),
            P(("groups", "dp"), None, "seq", "mp"),
            P(None, "mp"),
            P("mp"),
            P(("groups", "dp"), None),
            P(("groups", "dp"), "seq", None),
        ),
        out_specs=(P(("groups", "dp"), "seq", None, "mp"), P(("groups", "seq", "dp"), "mp")),
        check_vma=False,
    )
```

```python
import functools
import math

import jax
import jax.numpy as jnp
from jax import lax
from jax.experimental import pallas as pl
from jax.experimental.pallas import tpu as pltpu
from jax.sharding import PartitionSpec as P

inv_root_two = 0.7071067811865476
inv_root_tau = 0.3989422804014327
bf16, f32, i32 = jnp.bfloat16, jnp.float32, jnp.int32
vmem = pl.BlockSpec(memory_space=pltpu.VMEM)
smem = pl.BlockSpec(memory_space=pltpu.SMEM)
hbm = pl.BlockSpec(memory_space=pltpu.HBM)


def call(body, outs, in_specs, scratch=(), flops=0, moved=0, exps=0, vmem_mib=40):
    return pl.pallas_call(
        body,
        out_shape=outs,
        in_specs=in_specs,
        out_specs=[vmem] * len(outs),
        scratch_shapes=list(scratch),
        compiler_params=pltpu.CompilerParams(vmem_limit_bytes=vmem_mib << 20),
        cost_estimate=pl.CostEstimate(flops=flops, bytes_accessed=moved, transcendentals=exps),
    )


def shape(dtype, *extent):
    return jax.ShapeDtypeStruct(extent, dtype)


def exchanged(array, axis, distance):
    return lax.ppermute(array, axis, [(i, i ^ distance) for i in range(lax.axis_size(axis))])


def gelu_slope(preact):
    return (
        0.5 * (1.0 + lax.erf(preact * inv_root_two))
        + preact * jnp.exp(-0.5 * preact * preact) * inv_root_tau
    )


def kept_before(count_ref, frame):
    total = jnp.int32(0)
    for index in range(count_ref.shape[1]):
        total += jnp.where(index < frame, count_ref[0, index], 0)
    return total


def slot_start(range_begin, source, seq_size, rows_dev, slot_rows):
    first_row = lax.div(range_begin - source + (seq_size - 1), jnp.int32(seq_size))
    return jnp.minimum(first_row, rows_dev - slot_rows)


def pack_kernel(seq_size, frames_dev, slot_rows, partner, count_hbm, grads_hbm, *refs):
    *outs, count_ref, grads_ref, count_sem, grads_sem = refs
    count_copy = pltpu.make_async_copy(count_hbm, count_ref, count_sem)
    grads_copy = pltpu.make_async_copy(grads_hbm, grads_ref, grads_sem)
    count_copy.start()
    grads_copy.start()
    count_copy.wait()
    my_seq = lax.axis_index("seq")
    rows_dev = grads_ref.shape[0]
    row = lax.broadcasted_iota(i32, (slot_rows, rows_dev), 0)
    column = lax.broadcasted_iota(i32, (slot_rows, rows_dev), 1)
    starts = []
    for k in range(seq_size):
        begin = kept_before(count_ref, partner(my_seq, k) * frames_dev)
        starts.append(slot_start(begin, my_seq, seq_size, rows_dev, slot_rows))
    grads_copy.wait()
    for k, start in enumerate(starts):
        picks = jnp.where(column == row + start, 1.0, 0.0).astype(bf16)
        rows = jnp.dot(picks, grads_ref[...], preferred_element_type=f32).astype(bf16)
        if len(outs) == 1:
            outs[0][k] = rows
        else:
            outs[k][...] = rows


def slope_kernel(
    seq_size, rows_dev, slot_rows, partner, count_ref, order_ref, tokens_ref, weight_ref, bias_ref,
    slope_ref, rows_t_ref, place_ref, slot_pos, token_pos, rows_ref,
):
    my_seq = lax.axis_index("seq")
    frames_dev, patches = order_ref.shape
    tokens, width = tokens_ref.shape
    slots = slope_ref.shape[0]
    range_begin = kept_before(count_ref, my_seq * frames_dev)
    step = lax.broadcasted_iota(i32, (slot_rows, 1), 0)
    lane = lax.broadcasted_iota(i32, (1, slots), 1)
    slot_row = jnp.zeros((1, slots), i32)
    for k in range(seq_size):
        source = partner(my_seq, k)
        start = slot_start(range_begin, source, seq_size, rows_dev, slot_rows)
        slot_pos[k * slot_rows:(k + 1) * slot_rows, :] = (start + step) * seq_size + source
        slot_row = jnp.where(lane >= k * slot_rows, (start + lane - k * slot_rows) * seq_size + source, slot_row)
    token = lax.broadcasted_iota(i32, (patches, patches), 0)
    index = lax.broadcasted_iota(i32, (patches, patches), 1)
    begin = range_begin
    for frame in range(frames_dev):
        count = count_ref[0, my_seq * frames_dev + frame]
        order = order_ref[frame:frame + 1, :]
        rank = jnp.sum(jnp.where(order == token, index, 0), axis=1, keepdims=True)
        token_pos[frame * patches:(frame + 1) * patches, :] = jnp.where(rank < count, rank + begin, -1)
        begin += count
    column = token_pos[...]
    place_ref[...] = jnp.where(column == slot_row, 1.0, 0.0).astype(bf16)
    row = lax.broadcasted_iota(i32, (tokens, tokens), 0)
    lane = lax.broadcasted_iota(i32, (tokens, tokens), 1)
    token_row = jnp.sum(jnp.where(row == lane, column, 0), axis=0, keepdims=True)
    block = slots // 4

    @pl.loop(0, 4)
    def _(part):
        here = pl.ds(pl.multiple_of(part * block, 16), block)
        picks = jnp.where(slot_pos[here, :] == token_row, 1.0, 0.0).astype(bf16)
        rows = jnp.dot(picks, tokens_ref[...], preferred_element_type=f32).astype(bf16)
        rows_ref[here, :] = rows
        preact = jnp.dot(rows, weight_ref[...], preferred_element_type=f32) + bias_ref[...]
        slope_ref[here, :] = gelu_slope(preact)

    rows_t_ref[...] = rows_ref[...].T


def grad_kernel(slots_in, chunks, tile, *refs):
    grads, (slope_ref, rows_t_ref, grad_ref), outs = refs[:slots_in], refs[slots_in:slots_in + 3], refs[slots_in + 3:]
    slot_rows = grads[0].shape[0]
    for k, ref in enumerate(grads):
        here = slice(k * slot_rows, (k + 1) * slot_rows)
        grad_ref[here, :] = (ref[...].astype(f32) * slope_ref[here, :]).astype(bf16)
    weight_rows(chunks, tile, rows_t_ref, grad_ref, outs)


def weight_rows(chunks, tile, rows_t_ref, grad_ref, outs):
    my_seq, my_dp = lax.axis_index("seq"), lax.axis_index("dp")
    videos = lax.axis_size("dp")
    for (k, j), ref in zip(chunks, outs):
        owner = (my_seq ^ k) * videos + (my_dp ^ j)
        rows = rows_t_ref[pl.ds(pl.multiple_of(owner * tile, 16), tile), :]
        ref[...] = jnp.dot(rows, grad_ref[...], preferred_element_type=f32).astype(ref.dtype)


def rest_kernel(chunks, tile, rows_t_ref, grad_ref, weight_ref, own_ref, peer_ref, *outs):
    weight_rows(chunks, tile, rows_t_ref, grad_ref, outs)
    my_half = lax.axis_index("mp")
    half = own_ref.shape[1]
    for ref, which in ((peer_ref, 1 - my_half), (own_ref, my_half)):
        part = weight_ref[pl.ds(pl.multiple_of(which * half, 16), half), :]
        rows = lax.dot_general(grad_ref[...], part, (((1,), (1,)), ((), ())), preferred_element_type=f32)
        ref[...] = rows.astype(ref.dtype)


def place_kernel(own_ref, peer_ref, place_ref, out_ref):
    rows = (own_ref[...] + peer_ref[...].astype(f32)).astype(bf16)
    out_ref[...] = jnp.dot(place_ref[...], rows, preferred_element_type=f32).astype(bf16)


def shards(features, hidden_grad, weight, bias, keep_count, keep_order):
    seq_size, videos = lax.axis_size("seq"), lax.axis_size("dp")
    frames_dev, patches, width = features.shape[1:]
    rows_dev, hidden = hidden_grad.shape[1], hidden_grad.shape[3]
    tokens = frames_dev * patches
    slot_rows = (tokens + seq_size - 1) // seq_size
    slot_rows = (slot_rows + 15) // 16 * 16
    slots = seq_size * slot_rows
    tile = width // (seq_size * videos)
    direct = seq_size == 4 and videos == 2 and tile % 16 == 0
    norm_scale = 1.0 / math.sqrt(videos * seq_size * rows_dev)

    def partner(me, k):
        return me ^ k if direct else jnp.int32(k)

    local_grads = hidden_grad.reshape(rows_dev, hidden)
    flat_tokens = features.reshape(tokens, width)
    one = shape(bf16, slot_rows, hidden)
    outgoing = call(
        functools.partial(pack_kernel, seq_size, frames_dev, slot_rows, partner),
        [one] * seq_size if direct else [shape(bf16, seq_size, slot_rows, hidden)],
        [hbm, hbm],
        [
            pltpu.SMEM(keep_count.shape, i32),
            pltpu.VMEM((rows_dev, hidden), bf16),
            pltpu.SemaphoreType.DMA(()),
            pltpu.SemaphoreType.DMA(()),
        ],
        vmem_mib=60,
        flops=2 * slots * rows_dev * hidden,
        moved=2 * hidden * (rows_dev + slots),
    )(keep_count, local_grads)
    if direct:
        arrived = [exchanged(outgoing[k], "seq", k) for k in range(seq_size - 1, 0, -1)] + [outgoing[0]]
        arrived = arrived[::-1]
    else:
        arrived = [lax.all_to_all(outgoing[0], "seq", split_axis=0, concat_axis=0, tiled=True).reshape(slots, hidden)]

    slope, rows_t, place = call(
        functools.partial(slope_kernel, seq_size, rows_dev, slot_rows, partner),
        [shape(f32, slots, hidden), shape(bf16, width, slots), shape(bf16, tokens, slots)],
        [smem, vmem, vmem, vmem, vmem],
        [pltpu.VMEM((slots, 1), i32), pltpu.VMEM((tokens, 1), i32), pltpu.VMEM((slots, width), bf16)],
        flops=2 * slots * width * (tokens + hidden),
        moved=2 * width * (tokens + hidden + slots) + 4 * slots * hidden,
        exps=2 * slots * hidden,
    )(keep_count, keep_order.reshape(frames_dev, patches), flat_tokens, weight, bias.reshape(1, hidden))

    half = width // lax.axis_size("mp")
    early, late = ((3, 2), (1, 0)) if direct else ((), ())

    def both(tiles):
        chunks = [(k, j) for j in (1, 0) for k in tiles]
        outs = [shape(bf16 if j else f32, tile, hidden) for _, j in chunks]
        return chunks, outs, 2 * sum(out.size for out in outs) * slots

    chunks, outs, flops = both(early)
    slope_grad, *first = call(
        functools.partial(grad_kernel, len(arrived), chunks, tile),
        [shape(bf16, slots, hidden), *outs],
        [vmem] * (len(arrived) + 2),
        flops=flops,
        moved=8 * slots * hidden + 2 * slots * width,
    )(*arrived, slope, rows_t)
    chunks, outs, flops = both(late)
    own_part, peer_part, *rest = call(
        functools.partial(rest_kernel, chunks, tile),
        [shape(f32, slots, half), shape(bf16, slots, half), *outs],
        [vmem] * 3,
        flops=flops + 2 * slots * width * hidden,
        moved=2 * hidden * (slots + width) + 3 * slots * width,
    )(rows_t, slope_grad, weight)
    peer_part = exchanged(peer_part, "mp", 1)
    (grid,) = call(
        place_kernel,
        [shape(bf16, tokens, half)],
        [vmem] * 3,
        flops=2 * tokens * slots * half,
        moved=2 * tokens * (slots + half) + 8 * slots * half,
    )(own_part, peer_part, place)
    if direct:
        far_out, second_out, far, second = first
        near_out, home_out, near, home = rest
        got, near_out = lax.optimization_barrier((exchanged(far_out, "dp", 1), near_out))
        relayed = exchanged((far + got.astype(f32)).astype(bf16), "seq", 1).astype(f32)
        got, home_out = lax.optimization_barrier((exchanged(second_out, "dp", 1), home_out))
        second = exchanged((second + got.astype(f32) + relayed).astype(bf16), "seq", 2)
        near = exchanged((near + exchanged(near_out, "dp", 1).astype(f32)).astype(bf16), "seq", 1)
        home = home + exchanged(home_out, "dp", 1).astype(f32)
        home, grid = lax.optimization_barrier((home, grid))
        summed = home + second.astype(f32) + near.astype(f32)
    else:
        partial = jnp.dot(rows_t, slope_grad, preferred_element_type=f32)
        summed = lax.psum_scatter(partial, ("seq", "dp"), scatter_dimension=0, tiled=True)
    return (grid.reshape(1, frames_dev, patches, half), summed * norm_scale)


def solution(mesh):
    return jax.shard_map(
        shards,
        mesh=mesh,
        in_specs=(
            P(("groups", "dp"), "seq", None, None),
            P(("groups", "dp"), None, "seq", "mp"),
            P(None, "mp"),
            P("mp"),
            P(("groups", "dp"), None),
            P(("groups", "dp"), "seq", None),
        ),
        out_specs=(P(("groups", "dp"), "seq", None, "mp"), P(("groups", "seq", "dp"), "mp")),
        check_vma=False,
    )
```

```python
import functools
import math

import jax
import jax.numpy as jnp
from jax import lax
from jax.experimental import pallas as pl
from jax.experimental.pallas import tpu as pltpu
from jax.sharding import PartitionSpec as P

inv_root_two = 0.7071067811865476
inv_root_tau = 0.3989422804014327
bf16, f32, i32 = jnp.bfloat16, jnp.float32, jnp.int32
vmem = pl.BlockSpec(memory_space=pltpu.VMEM)
smem = pl.BlockSpec(memory_space=pltpu.SMEM)
hbm = pl.BlockSpec(memory_space=pltpu.HBM)


def call(body, outs, in_specs, scratch=(), flops=0, moved=0, exps=0, vmem_mib=40):
    return pl.pallas_call(
        body,
        out_shape=outs,
        in_specs=in_specs,
        out_specs=[vmem] * len(outs),
        scratch_shapes=list(scratch),
        compiler_params=pltpu.CompilerParams(vmem_limit_bytes=vmem_mib << 20),
        cost_estimate=pl.CostEstimate(flops=flops, bytes_accessed=moved, transcendentals=exps),
    )


def shape(dtype, *extent):
    return jax.ShapeDtypeStruct(extent, dtype)


def exchanged(array, axis, distance):
    return lax.ppermute(array, axis, [(i, i ^ distance) for i in range(lax.axis_size(axis))])


def gelu_slope(preact):
    return (
        0.5 * (1.0 + lax.erf(preact * inv_root_two))
        + preact * jnp.exp(-0.5 * preact * preact) * inv_root_tau
    )


def kept_before(count_ref, frame):
    total = jnp.int32(0)
    for index in range(count_ref.shape[1]):
        total += jnp.where(index < frame, count_ref[0, index], 0)
    return total


def slot_start(range_begin, source, seq_size, rows_dev, slot_rows):
    first_row = lax.div(range_begin - source + (seq_size - 1), jnp.int32(seq_size))
    return jnp.minimum(first_row, rows_dev - slot_rows)


def pack_kernel(seq_size, frames_dev, slot_rows, partner, count_hbm, grads_hbm, *refs):
    *outs, count_ref, grads_ref, count_sem, grads_sem = refs
    count_copy = pltpu.make_async_copy(count_hbm, count_ref, count_sem)
    grads_copy = pltpu.make_async_copy(grads_hbm, grads_ref, grads_sem)
    count_copy.start()
    grads_copy.start()
    count_copy.wait()
    my_seq = lax.axis_index("seq")
    rows_dev = grads_ref.shape[0]
    row = lax.broadcasted_iota(i32, (slot_rows, rows_dev), 0)
    column = lax.broadcasted_iota(i32, (slot_rows, rows_dev), 1)
    starts = []
    for k in range(seq_size):
        begin = kept_before(count_ref, partner(my_seq, k) * frames_dev)
        starts.append(slot_start(begin, my_seq, seq_size, rows_dev, slot_rows))
    grads_copy.wait()
    for k, start in enumerate(starts):
        picks = jnp.where(column == row + start, 1.0, 0.0).astype(bf16)
        rows = jnp.dot(picks, grads_ref[...], preferred_element_type=f32).astype(bf16)
        if len(outs) == 1:
            outs[0][k] = rows
        else:
            outs[k][...] = rows


def slope_kernel(
    seq_size, rows_dev, slot_rows, partner, count_ref, order_ref, tokens_ref, weight_ref, bias_ref,
    slope_ref, rows_t_ref, place_ref, slot_pos, token_pos, rows_ref,
):
    my_seq = lax.axis_index("seq")
    frames_dev, patches = order_ref.shape
    tokens, width = tokens_ref.shape
    slots = slope_ref.shape[0]
    range_begin = kept_before(count_ref, my_seq * frames_dev)
    step = lax.broadcasted_iota(i32, (slot_rows, 1), 0)
    lane = lax.broadcasted_iota(i32, (1, slots), 1)
    slot_row = jnp.zeros((1, slots), i32)
    for k in range(seq_size):
        source = partner(my_seq, k)
        start = slot_start(range_begin, source, seq_size, rows_dev, slot_rows)
        slot_pos[k * slot_rows:(k + 1) * slot_rows, :] = (start + step) * seq_size + source
        slot_row = jnp.where(lane >= k * slot_rows, (start + lane - k * slot_rows) * seq_size + source, slot_row)
    token = lax.broadcasted_iota(i32, (patches, patches), 0)
    index = lax.broadcasted_iota(i32, (patches, patches), 1)
    begin = range_begin
    for frame in range(frames_dev):
        count = count_ref[0, my_seq * frames_dev + frame]
        order = order_ref[frame:frame + 1, :]
        rank = jnp.sum(jnp.where(order == token, index, 0), axis=1, keepdims=True)
        token_pos[frame * patches:(frame + 1) * patches, :] = jnp.where(rank < count, rank + begin, -1)
        begin += count
    column = token_pos[...]
    place_ref[...] = jnp.where(column == slot_row, 1.0, 0.0).astype(bf16)
    row = lax.broadcasted_iota(i32, (tokens, tokens), 0)
    lane = lax.broadcasted_iota(i32, (tokens, tokens), 1)
    token_row = jnp.sum(jnp.where(row == lane, column, 0), axis=0, keepdims=True)
    block = slots // 4

    @pl.loop(0, 4)
    def _(part):
        here = pl.ds(pl.multiple_of(part * block, 16), block)
        picks = jnp.where(slot_pos[here, :] == token_row, 1.0, 0.0).astype(bf16)
        rows = jnp.dot(picks, tokens_ref[...], preferred_element_type=f32).astype(bf16)
        rows_ref[here, :] = rows
        preact = jnp.dot(rows, weight_ref[...], preferred_element_type=f32) + bias_ref[...]
        slope_ref[here, :] = gelu_slope(preact)

    rows_t_ref[...] = rows_ref[...].T


def grad_kernel(slots_in, chunks, tile, *refs):
    grads, (slope_ref, rows_t_ref, grad_ref), outs = refs[:slots_in], refs[slots_in:slots_in + 3], refs[slots_in + 3:]
    slot_rows = grads[0].shape[0]
    for k, ref in enumerate(grads):
        here = slice(k * slot_rows, (k + 1) * slot_rows)
        grad_ref[here, :] = (ref[...].astype(f32) * slope_ref[here, :]).astype(bf16)
    weight_rows(chunks, tile, rows_t_ref, grad_ref, outs)


def weight_rows(chunks, tile, rows_t_ref, grad_ref, outs):
    my_seq, my_dp = lax.axis_index("seq"), lax.axis_index("dp")
    videos = lax.axis_size("dp")
    for (k, j), ref in zip(chunks, outs):
        owner = (my_seq ^ k) * videos + (my_dp ^ j)
        rows = rows_t_ref[pl.ds(pl.multiple_of(owner * tile, 16), tile), :]
        ref[...] = jnp.dot(rows, grad_ref[...], preferred_element_type=f32).astype(ref.dtype)


def rest_kernel(chunks, tile, rows_t_ref, grad_ref, weight_ref, own_ref, peer_ref, *outs):
    weight_rows(chunks, tile, rows_t_ref, grad_ref, outs)
    my_half = lax.axis_index("mp")
    half = own_ref.shape[1]
    for ref, which in ((peer_ref, 1 - my_half), (own_ref, my_half)):
        part = weight_ref[pl.ds(pl.multiple_of(which * half, 16), half), :]
        rows = lax.dot_general(grad_ref[...], part, (((1,), (1,)), ((), ())), preferred_element_type=f32)
        ref[...] = rows.astype(ref.dtype)


def place_kernel(own_ref, peer_ref, place_ref, out_ref):
    rows = (own_ref[...] + peer_ref[...].astype(f32)).astype(bf16)
    out_ref[...] = jnp.dot(place_ref[...], rows, preferred_element_type=f32).astype(bf16)


def shards(features, hidden_grad, weight, bias, keep_count, keep_order):
    seq_size, videos = lax.axis_size("seq"), lax.axis_size("dp")
    frames_dev, patches, width = features.shape[1:]
    rows_dev, hidden = hidden_grad.shape[1], hidden_grad.shape[3]
    tokens = frames_dev * patches
    slot_rows = (tokens + seq_size - 1) // seq_size
    slot_rows = (slot_rows + 15) // 16 * 16
    slots = seq_size * slot_rows
    tile = width // (seq_size * videos)
    direct = seq_size == 4 and videos == 2 and tile % 16 == 0
    norm_scale = 1.0 / math.sqrt(videos * seq_size * rows_dev)

    def partner(me, k):
        return me ^ k if direct else jnp.int32(k)

    local_grads = hidden_grad.reshape(rows_dev, hidden)
    flat_tokens = features.reshape(tokens, width)
    one = shape(bf16, slot_rows, hidden)
    outgoing = call(
        functools.partial(pack_kernel, seq_size, frames_dev, slot_rows, partner),
        [one] * seq_size if direct else [shape(bf16, seq_size, slot_rows, hidden)],
        [hbm, hbm],
        [
            pltpu.SMEM(keep_count.shape, i32),
            pltpu.VMEM((rows_dev, hidden), bf16),
            pltpu.SemaphoreType.DMA(()),
            pltpu.SemaphoreType.DMA(()),
        ],
        vmem_mib=60,
        flops=2 * slots * rows_dev * hidden,
        moved=2 * hidden * (rows_dev + slots),
    )(keep_count, local_grads)
    if direct:
        arrived = [exchanged(outgoing[k], "seq", k) for k in range(seq_size - 1, 0, -1)] + [outgoing[0]]
        arrived = arrived[::-1]
    else:
        arrived = [lax.all_to_all(outgoing[0], "seq", split_axis=0, concat_axis=0, tiled=True).reshape(slots, hidden)]

    slope, rows_t, place = call(
        functools.partial(slope_kernel, seq_size, rows_dev, slot_rows, partner),
        [shape(f32, slots, hidden), shape(bf16, width, slots), shape(bf16, tokens, slots)],
        [smem, vmem, vmem, vmem, vmem],
        [pltpu.VMEM((slots, 1), i32), pltpu.VMEM((tokens, 1), i32), pltpu.VMEM((slots, width), bf16)],
        flops=2 * slots * width * (tokens + hidden),
        moved=2 * width * (tokens + hidden + slots) + 4 * slots * hidden,
        exps=2 * slots * hidden,
    )(keep_count, keep_order.reshape(frames_dev, patches), flat_tokens, weight, bias.reshape(1, hidden))

    half = width // lax.axis_size("mp")
    early = [(3, 1), (2, 1)] if direct else []
    late = [(1, 1), (0, 1), (3, 0), (2, 0), (1, 0), (0, 0)] if direct else []

    def tiles_of(chunks):
        outs = [shape(bf16 if j else f32, tile, hidden) for _, j in chunks]
        return outs, 2 * sum(out.size for out in outs) * slots

    outs, flops = tiles_of(early)
    slope_grad, *first = call(
        functools.partial(grad_kernel, len(arrived), early, tile),
        [shape(bf16, slots, hidden), *outs],
        [vmem] * (len(arrived) + 2),
        flops=flops,
        moved=8 * slots * hidden + 2 * slots * width,
    )(*arrived, slope, rows_t)
    outs, flops = tiles_of(late)
    own_part, peer_part, *rest = call(
        functools.partial(rest_kernel, late, tile),
        [shape(f32, slots, half), shape(bf16, slots, half), *outs],
        [vmem] * 3,
        flops=flops + 2 * slots * width * hidden,
        moved=2 * hidden * (slots + width) + 3 * slots * width,
    )(rows_t, slope_grad, weight)
    peer_part = exchanged(peer_part, "mp", 1)
    (grid,) = call(
        place_kernel,
        [shape(bf16, tokens, half)],
        [vmem] * 3,
        flops=2 * tokens * slots * half,
        moved=2 * tokens * (slots + half) + 8 * slots * half,
    )(own_part, peer_part, place)
    if direct:
        far_out, second_out = first
        near_out, home_out, far, second, near, home = rest
        got, near_out = lax.optimization_barrier((exchanged(far_out, "dp", 1), near_out))
        relayed = exchanged((far + got.astype(f32)).astype(bf16), "seq", 1).astype(f32)
        got, home_out = lax.optimization_barrier((exchanged(second_out, "dp", 1), home_out))
        second = exchanged((second + got.astype(f32) + relayed).astype(bf16), "seq", 2)
        near = exchanged((near + exchanged(near_out, "dp", 1).astype(f32)).astype(bf16), "seq", 1)
        home = home + exchanged(home_out, "dp", 1).astype(f32)
        home, grid = lax.optimization_barrier((home, grid))
        summed = home + second.astype(f32) + near.astype(f32)
    else:
        partial = jnp.dot(rows_t, slope_grad, preferred_element_type=f32)
        summed = lax.psum_scatter(partial, ("seq", "dp"), scatter_dimension=0, tiled=True)
    return (grid.reshape(1, frames_dev, patches, half), summed * norm_scale)


def solution(mesh):
    return jax.shard_map(
        shards,
        mesh=mesh,
        in_specs=(
            P(("groups", "dp"), "seq", None, None),
            P(("groups", "dp"), None, "seq", "mp"),
            P(None, "mp"),
            P("mp"),
            P(("groups", "dp"), None),
            P(("groups", "dp"), "seq", None),
        ),
        out_specs=(P(("groups", "dp"), "seq", None, "mp"), P(("groups", "seq", "dp"), "mp")),
        check_vma=False,
    )
```
